32 devices in a mesh: dp: 8 (over z, core), seq: 4 (over y, x).
Axes of the slice: x: 2, y: 2, z: 4, core: 2. Of those that a mesh axis runs over, the one named last changes fastest.
Arguments:
- tokens_in: float32 [16, 1024, 768], P('dp', 'seq'), may hold values from -6 to 6
- out_grad: float32 [16, 1024, 768], P('dp', 'seq'), may hold values from -6 to 6
- norm_gains: float32 [2304], P(('dp', 'seq')), may hold values from 0.1 to 1.9
- in_weight: float32 [768, 3352], P(('dp', 'seq')), may hold values from -0.21875 to 0.21875
- conv_weight: float32 [5, 1792], P(None, ('dp', 'seq')), may hold values from -3 to 3
- head_params: float32 [3, 24], replicated, may hold values from -8 to 4, as said below
- out_weight: float32 [1536, 768], P(None, ('dp', 'seq')), may hold values from -0.15625 to 0.15625
- gains_first: float32 [2304], P(('dp', 'seq')), may hold values from -40 to 40
- gains_second: float32 [2304], P(('dp', 'seq')), may hold values from 4.1001 to 16.4004
- in_first: float32 [768, 3352], P(('dp', 'seq')), may hold values from -24 to 24
- in_second: float32 [768, 3352], P(('dp', 'seq')), may hold values from 1.4760361 to 5.9041443
- conv_first: float32 [5, 1792], P(None, ('dp', 'seq')), may hold values from -16 to 16
- conv_second: float32 [5, 1792], P(None, ('dp', 'seq')), may hold values from 0.656016 to 2.624064
- head_first: float32 [3, 24], replicated, may hold values from -80 to 80
- head_second: float32 [3, 24], replicated, may hold values from 16.4004 to 65.6016
- out_first: float32 [1536, 768], P(None, ('dp', 'seq')), may hold values from -80 to 80
- out_second: float32 [1536, 768], P(None, ('dp', 'seq')), may hold values from 16.4004 to 65.6016
Outputs:
- block_out: float32 [16, 1024, 768], P('dp', 'seq')
- tokens_grad: float32 [16, 1024, 768], P('dp', 'seq')
- gains_first_new: float32 [2304], P(('dp', 'seq'))
- gains_second_new: float32 [2304], P(('dp', 'seq'))
- gains_new: float32 [2304], P(('dp', 'seq'))
- in_first_new: float32 [768, 3352], P(('dp', 'seq'))
- in_second_new: float32 [768, 3352], P(('dp', 'seq'))
- in_weight_new: float32 [768, 3352], P(('dp', 'seq'))
- conv_first_new: float32 [5, 1792], P(None, ('dp', 'seq'))
- conv_second_new: float32 [5, 1792], P(None, ('dp', 'seq'))
- conv_new: float32 [5, 1792], P(None, ('dp', 'seq'))
- head_first_new: float32 [3, 24], replicated
- head_second_new: float32 [3, 24], replicated
- head_new: float32 [3, 24], replicated
- out_first_new: float32 [1536, 768], P(None, ('dp', 'seq'))
- out_second_new: float32 [1536, 768], P(None, ('dp', 'seq'))
- out_weight_new: float32 [1536, 768], P(None, ('dp', 'seq'))
The draws below stay inside these ranges and needn't reach their ends.
Inputs may be any that keep to these rules, and one draw needn't show every extreme that they name: `head_params`: row 0 is log(exp(b) - 1) for a base step b of each head; row 1 is the logarithm of each head's decay rate; row 2 the skip coefficients.
All inputs are finite; a program needn't handle non-finite values.
Results may differ from the reference program's by a relative error of at most 0.012.
The reference program's roundings to bfloat16 on the way count: a program that leaves them out, or rounds other values in their place, can miss the bound.
Values may be sent and summed in bfloat16 or wider, within the bound.
A program may use at most 192 MiB of HBM per device.

```python
import math
import jax
import jax.numpy as jnp
from jax import lax

D = 768
H = 24
P_SIZE = 64
N = 128
CONV = 4
Q = 256
STEP = 10
DI = 1536
CD = 1792
E = 3352
LEN = 1024
SEQ_ALL = 16
TOKENS = 16384


def draw_head_params(key, part):
    key = jax.random.fold_in(key, 11)
    key_base, key_rate, key_skip = jax.random.split(key, 3)
    step_base = jnp.exp(jax.random.uniform(key_base, (H,), jnp.float32, jnp.log(0.001), jnp.log(0.1)))
    decay_speed = jnp.exp(jax.random.uniform(key_rate, (H,), jnp.float32, jnp.log(0.5 / LEN), jnp.log(1.0 / 30.0)))
    skip_gain = jax.random.uniform(key_skip, (H,), jnp.float32, 0.5, 1.5)
    bias_row = jnp.log(jnp.expm1(step_base))
    return jnp.stack([bias_row, jnp.log(decay_speed / step_base), skip_gain]).astype(jnp.float32)


def steps_of(key, dims, cuts, least, high):
    level, own = 1.0, jax.random.fold_in(key, 6)
    for position, blocks in cuts:
        steps = jnp.exp(jax.random.uniform(jax.random.fold_in(own, position), (blocks,), jnp.float32, least / len(cuts), high / len(cuts)))
        level = level * jnp.repeat(steps, dims[position] // blocks).reshape([-1 if axis == position else 1 for axis in range(len(dims))])
    return level


def centred(own_key, dims, spread, bound, shards=(), dtype=jnp.bfloat16):
    drawn = spread * jax.random.normal(own_key, dims, jnp.float32)
    if shards:
        drawn = drawn * steps_of(own_key, dims, shards, -0.22, 0.18)
    return jnp.clip(drawn, -bound, bound).astype(dtype)


def setup_inputs(seed: int = 0) -> dict:
    splits = jax.random.split(jax.random.key(seed), 18)
    return {
        "tokens_in": centred(splits[0], (SEQ_ALL, LEN, D), 1.0, 6.0, ((0, 8), (1, 4)), jnp.float32),
        "out_grad": centred(splits[1], (SEQ_ALL, LEN, D), 1.0, 6.0, ((0, 8), (1, 4)), jnp.float32),
        "norm_gains": jnp.clip(1.0 + 0.18 * jax.random.normal(splits[2], (D + DI,), jnp.float32), 0.1, 1.9),
        "in_weight": centred(splits[3], (D, E), D ** -0.5, 0.21875, ((0, 32),), jnp.float32),
        "conv_weight": centred(splits[4], (CONV + 1, CD), CONV ** -0.5, 3.0, ((1, 32),), jnp.float32),
        "head_params": draw_head_params(jax.random.fold_in(splits[17], 71), 0),
        "out_weight": centred(splits[6], (DI, D), DI ** -0.5, 0.15625, ((1, 32),), jnp.float32),
        "gains_first": centred(splits[7], (D + DI,), (0.5 * TOKENS ** 0.5 / 9), 40.0, ((0, 32),), jnp.float32),
        "gains_second": jnp.clip(jnp.exp(math.log(16.4004) - 1.3862944 * jax.random.uniform(splits[8], (D + DI,), jnp.float32) ** steps_of(splits[8], (D + DI,), ((0, 32),), -0.2, 0.2)), 4.1001, 16.4004),
        "in_first": centred(splits[9], (D, E), (0.3 * TOKENS ** 0.5 / 9), 24.0, ((0, 32),), jnp.float32),
        "in_second": jnp.clip(jnp.exp(math.log(5.9041443) - 1.3862944 * jax.random.uniform(splits[10], (D, E), jnp.float32) ** steps_of(splits[10], (D, E), ((0, 32),), -0.2, 0.2)), 1.4760361, 5.9041443),
        "conv_first": centred(splits[11], (CONV + 1, CD), (0.2 * TOKENS ** 0.5 / 9), 16.0, ((1, 32),), jnp.float32),
        "conv_second": jnp.clip(jnp.exp(math.log(2.624064) - 1.3862944 * jax.random.uniform(splits[12], (CONV + 1, CD), jnp.float32) ** steps_of(splits[12], (CONV + 1, CD), ((1, 32),), -0.2, 0.2)), 0.656016, 2.624064),
        "head_first": centred(splits[13], (3, H), (TOKENS ** 0.5 / 9), 80.0, (), jnp.float32),
        "head_second": jnp.clip(jnp.exp(jax.random.uniform(splits[14], (3, H), jnp.float32, math.log(16.4004), math.log(65.6016))), 16.4004, 65.6016),
        "out_first": centred(splits[15], (DI, D), (TOKENS ** 0.5 / 9), 80.0, ((1, 32),), jnp.float32),
        "out_second": jnp.clip(jnp.exp(math.log(65.6016) - 1.3862944 * jax.random.uniform(splits[16], (DI, D), jnp.float32) ** steps_of(splits[16], (DI, D), ((1, 32),), -0.2, 0.2)), 16.4004, 65.6016),
    }


@jax.custom_vjp
def low(v):
    return lax.optimization_barrier(v.astype(jnp.bfloat16)).astype(jnp.float32)

@jax.custom_vjp
def low_back(v):
    return v

def low_keep(v):
    return (low(v), None)

def low_pass(kept, grad):
    return (grad,)

def back_keep(v):
    return (v, None)

def back_low(kept, grad):
    return (low(grad),)
low.defvjp(low_keep, low_pass)
low_back.defvjp(back_keep, back_low)
norm_eps = 1e-05
beta_one = 0.9
beta_two = 0.999
adam_eps = 1e-08
decay_rate = 0.01
rate_gains = 0.25
rate_in = 0.04
rate_conv = 0.4
rate_heads = 0.6
rate_out = 0.03

def matmul_high(left, right):
    return jnp.dot(left, right, precision=lax.Precision.HIGHEST, preferred_element_type=jnp.float32)

def rms_scale(values, gain):
    return values * lax.rsqrt(lax.optimization_barrier(jnp.mean(values * values, axis=-1, keepdims=True)) + norm_eps) * gain

def block_step(carry_state, pieces, head_decay, skip_gain):
    head_in, b_input, c_output, step_size = pieces
    cumulative = jnp.cumsum(step_size * head_decay, axis=0)
    row_index = lax.broadcasted_iota(jnp.int32, (Q, Q), 0)
    col_index = lax.broadcasted_iota(jnp.int32, (Q, Q), 1)
    causal = (col_index <= row_index)[:, :, None]
    log_decay = cumulative[:, None, :] - cumulative[None, :, :]
    decay_mask = jnp.exp(jnp.where(causal, log_decay, -1e+30))
    inner_bc = matmul_high(c_output, b_input.T)
    mixing = inner_bc[:, :, None] * decay_mask * step_size[None, :, :]
    intra_out = jnp.einsum('tsh,shp->thp', mixing, head_in, precision=lax.Precision.HIGHEST)
    inter_out = jnp.exp(cumulative)[:, :, None] * jnp.einsum('tn,hpn->thp', c_output, carry_state, precision=lax.Precision.HIGHEST)
    weights_end = jnp.exp(cumulative[-1][None, :] - cumulative) * step_size
    local_state = jnp.einsum('shp,sn->hpn', weights_end[:, :, None] * head_in, b_input, precision=lax.Precision.HIGHEST)
    new_state = jnp.exp(cumulative[-1])[:, None, None] * carry_state + local_state
    return (new_state, intra_out + inter_out + skip_gain[None, :, None] * head_in)

def layer_forward(tokens, norm_gains, in_weight, conv_weight, head_params, out_weight):
    gain_all = low(norm_gains)
    normed = low(rms_scale(tokens, gain_all[:D]))
    projected = low(low_back(matmul_high(normed, low(in_weight))))
    gate_rows = projected[:, :DI]
    conv_in = projected[:, DI:DI + CD]
    step_raw = projected[:, DI + CD:]
    conv_taps = low(conv_weight)
    padded = jnp.concatenate([jnp.zeros((CONV - 1, CD), jnp.float32), conv_in], axis=0)
    conv_sum = conv_taps[CONV] + conv_taps[0] * padded[0:LEN]
    for offset in range(1, CONV):
        conv_sum = conv_sum + conv_taps[offset] * padded[offset:offset + LEN]
    mixed_in = low(jax.nn.silu(conv_sum))
    block_count = LEN // Q
    head_in = mixed_in[:, :DI].reshape(block_count, Q, H, P_SIZE)
    b_input = mixed_in[:, DI:DI + N].reshape(block_count, Q, N)
    c_output = mixed_in[:, DI + N:].reshape(block_count, Q, N)
    step_size = jax.nn.softplus(step_raw + head_params[0]).reshape(block_count, Q, H)
    head_decay = -jnp.exp(head_params[1])
    skip_gain = head_params[2]

    def advance(carry_state, pieces):
        return block_step(carry_state, pieces, head_decay, skip_gain)
    start_state = jnp.zeros((H, P_SIZE, N), jnp.float32)
    end_state, ssd_out = lax.scan(jax.checkpoint(advance), start_state, (head_in, b_input, c_output, step_size))
    gated = ssd_out.reshape(LEN, DI) * jax.nn.silu(gate_rows)
    mixed_out = low(rms_scale(gated, gain_all[D:]))
    branch = low_back(matmul_high(mixed_out, low(out_weight)))
    return tokens + branch

def adamw_update(weight, gradient, first_moment, second_moment, step_rate):
    first_next = beta_one * first_moment + (1.0 - beta_one) * gradient
    second_next = beta_two * second_moment + (1.0 - beta_two) * gradient * gradient
    first_hat = first_next / (1.0 - beta_one ** STEP)
    second_hat = second_next / (1.0 - beta_two ** STEP)
    weight_next = weight - step_rate * (first_hat / (jnp.sqrt(second_hat) + adam_eps) + decay_rate * weight)
    return (first_next, second_next, weight_next)

def reference(tokens_in, out_grad, norm_gains, in_weight, conv_weight, head_params, out_weight, gains_first, gains_second, in_first, in_second, conv_first, conv_second, head_first, head_second, out_first, out_second):
    params = (norm_gains, in_weight, conv_weight, head_params, out_weight)

    def one_sequence(totals, seq_pair):
        seq_tokens, seq_grad = seq_pair
        result, pullback = jax.vjp(layer_forward, seq_tokens, norm_gains, in_weight, conv_weight, head_params, out_weight)
        gradients = pullback(seq_grad)
        totals = tuple((running + addend for running, addend in zip(totals, gradients[1:])))
        return (totals, (result, gradients[0]))
    zero_grads = tuple((jnp.zeros_like(param_array) for param_array in params))
    totals, (block_out, tokens_grad) = lax.scan(one_sequence, zero_grads, (tokens_in, out_grad))
    gains_next = adamw_update(norm_gains, totals[0], gains_first, gains_second, rate_gains)
    in_next = adamw_update(in_weight, totals[1], in_first, in_second, rate_in)
    conv_next = adamw_update(conv_weight, totals[2], conv_first, conv_second, rate_conv)
    head_next = adamw_update(head_params, totals[3], head_first, head_second, rate_heads)
    out_next = adamw_update(out_weight, totals[4], out_first, out_second, rate_out)
    return (block_out, tokens_grad, gains_next[0], gains_next[1], gains_next[2], in_next[0], in_next[1], in_next[2], conv_next[0], conv_next[1], conv_next[2], head_next[0], head_next[1], head_next[2], out_next[0], out_next[1], out_next[2])
```

```python
import jax
import jax.numpy as jnp
from jax import lax
from jax.sharding import PartitionSpec as P

D = 768
H = 24
P_SIZE = 64
N = 128
CONV = 4
STEP = 10
DI = 1536
CD = 1792


norm_eps = 1e-05
beta_one = 0.9
beta_two = 0.999
adam_eps = 1e-08
decay_rate = 0.01
rate_gains = 0.25
rate_in = 0.04
rate_conv = 0.4
rate_heads = 0.6
rate_out = 0.03


def from_behind(value, axis, steps):
    count = lax.axis_size(axis)
    leading, last = (max(0, -steps), min(count, count - steps))
    return lax.ppermute(value, axis, [(source, source + steps) for source in range(leading, last)])


def earlier_sum(state, decays, axis):
    total, factor = (None, None)
    for steps, decay in decays:
        term = from_behind(state, axis, steps).astype(jnp.float32)
        total = term if total is None else total + factor[..., None, None] * term
        factor = decay if factor is None else factor * decay
    return total


def shared_sum(value, axes):
    for axis in axes:
        count, apart = (lax.axis_size(axis), 1)
        while apart < count:
            pairs = [(place, place ^ apart) for place in range(count)]
            value = value + lax.ppermute(value, axis, pairs)
            apart = apart * 2
    return value


def rounded(values):
    return lax.optimization_barrier(values.astype(jnp.bfloat16)).astype(jnp.float32)


def norm_apply(values, gain):
    return values * lax.rsqrt(jnp.mean(values * values, axis=-1, keepdims=True) + norm_eps) * gain


def gated_apply(ssd_out, gate_rows, gain):
    return norm_apply(ssd_out * jax.nn.silu(gate_rows), gain)


def conv_apply(extended, conv_taps):
    length = extended.shape[1] - (CONV - 1)
    conv_sum = conv_taps[CONV] + conv_taps[0] * extended[:, 0:length]
    for offset in range(1, CONV):
        conv_sum = conv_sum + conv_taps[offset] * extended[:, offset : offset + length]
    return jax.nn.silu(conv_sum)


def block_parts(step_raw, head_params):
    step_size = jax.nn.softplus(step_raw + head_params[0])
    length = step_raw.shape[1]
    row_index = lax.broadcasted_iota(jnp.int32, (length, length), 0)
    col_index = lax.broadcasted_iota(jnp.int32, (length, length), 1)
    until = (col_index <= row_index).astype(jnp.float32)
    cumulative = jnp.einsum(
        "ts,bsh->bth", until, step_size * -jnp.exp(head_params[1]), precision=lax.Precision.HIGHEST
    )
    return (step_size, cumulative)


def state_local(head_in, b_input, step_raw, head_params):
    step_size, cumulative = block_parts(step_raw, head_params)
    weights_end = jnp.exp(cumulative[:, -1:, :] - cumulative) * step_size
    local_state = jnp.einsum(
        "bshp,bsn->bhpn", weights_end[..., None] * head_in, b_input
    )
    return (jnp.exp(cumulative[:, -1, :]), local_state)


def block_output(head_in, b_input, c_output, step_raw, head_params, incoming):
    step_size, cumulative = block_parts(step_raw, head_params)
    length = head_in.shape[1]
    row_index = lax.broadcasted_iota(jnp.int32, (length, length), 0)
    col_index = lax.broadcasted_iota(jnp.int32, (length, length), 1)
    causal = (col_index <= row_index)[None, None]
    cum_heads = jnp.swapaxes(cumulative, 1, 2)
    log_decay = cum_heads[:, :, :, None] - cum_heads[:, :, None, :]
    decay_mask = jnp.exp(jnp.where(causal, log_decay, -1e30))
    inner_bc = jnp.einsum("btn,bsn->bts", c_output, b_input)
    mixing = inner_bc[:, None] * decay_mask * jnp.swapaxes(step_size, 1, 2)[:, :, None, :]
    intra_out = jnp.einsum("bhts,bshp->bthp", mixing, head_in)
    inter_out = jnp.exp(cumulative)[..., None] * jnp.einsum(
        "btn,bhpn->bthp", c_output, incoming
    )
    return intra_out + inter_out + head_params[2][:, None] * head_in


def fetch_weights(norm_gains, in_weight, conv_weight, out_weight):
    axes = ("dp", "seq")
    rows, wide = in_weight.shape
    own_gains = norm_gains.shape[0]
    own_taps = conv_weight.size
    columns = -(-(own_gains + own_taps) // rows)
    small = jnp.concatenate([norm_gains, conv_weight.reshape(-1)])
    small = jnp.pad(small, (0, rows * columns - small.shape[0])).reshape(rows, columns)
    packed = jnp.concatenate([in_weight, small], axis=1).astype(jnp.bfloat16)
    whole = lax.all_gather(packed, axes, axis=0, tiled=True)
    out_low = lax.all_gather(out_weight.astype(jnp.bfloat16).T, axes, axis=0, tiled=True)
    count = whole.shape[0] // rows
    small_all = whole[:, wide:].reshape(count, rows * columns)
    gain_all = small_all[:, :own_gains].reshape(-1)
    taps = small_all[:, own_gains : own_gains + own_taps].reshape(count, CONV + 1, -1)
    conv_taps = jnp.swapaxes(taps, 0, 1).reshape(CONV + 1, -1)
    return (gain_all, whole[:, :wide], conv_taps, out_low)


def adamw_update(weight, gradient, first_moment, second_moment, step_rate):
    first_next = beta_one * first_moment + (1.0 - beta_one) * gradient
    second_next = beta_two * second_moment + (1.0 - beta_two) * gradient * gradient
    first_hat = first_next / (1.0 - beta_one**STEP)
    second_hat = second_next / (1.0 - beta_two**STEP)
    weight_next = weight - step_rate * (
        first_hat / (jnp.sqrt(second_hat) + adam_eps) + decay_rate * weight
    )
    return (first_next, second_next, weight_next)


def body(
    tokens_in,
    out_grad,
    norm_gains,
    in_weight,
    conv_weight,
    head_params,
    out_weight,
    gains_first,
    gains_second,
    in_first,
    in_second,
    conv_first,
    conv_second,
    head_first,
    head_second,
    out_first,
    out_second,
):
    seq_count, length, model_width = tokens_in.shape
    tok_rows = seq_count * length
    fetched = fetch_weights(norm_gains, in_weight, conv_weight, out_weight)
    gain_all = fetched[0].astype(jnp.float32)
    in_low = fetched[1]
    conv_taps = fetched[2].astype(jnp.float32)
    out_low = fetched[3]
    gain_in = gain_all[:D]
    gain_mix = gain_all[D:]
    flat_tokens = tokens_in.reshape(tok_rows, model_width)
    normed = norm_apply(flat_tokens, gain_in).astype(jnp.bfloat16)
    projected = jnp.dot(normed, in_low, preferred_element_type=jnp.float32).astype(jnp.bfloat16)
    gate_rows = projected[:, :DI].astype(jnp.float32)
    conv_in = projected[:, DI : DI + CD].reshape(seq_count, length, CD)
    step_raw = projected[:, DI + CD :].astype(jnp.float32).reshape(seq_count, length, H)
    tail_rows = conv_in[:, length - (CONV - 1) :, :]
    before_rows = from_behind(tail_rows, "seq", 1)
    extended = jnp.concatenate([before_rows, conv_in], axis=1).astype(jnp.float32)
    mixed_in = rounded(conv_apply(extended, conv_taps))
    head_in = mixed_in[..., :DI].reshape(seq_count, length, H, P_SIZE)
    b_input = mixed_in[..., DI : DI + N]
    c_output = mixed_in[..., DI + N :]
    decay_end, local_state = state_local(head_in, b_input, step_raw, head_params)
    peers = lax.axis_size("seq")
    before = [(k, from_behind(decay_end, "seq", k)) for k in range(1, peers)]
    after = [(-k, from_behind(decay_end, "seq", -k)) for k in range(1, peers)]
    incoming = earlier_sum(local_state.astype(jnp.bfloat16), before, "seq")
    ssd_out = block_output(head_in, b_input, c_output, step_raw, head_params, incoming).reshape(
        tok_rows, DI
    )
    mixed_out = gated_apply(ssd_out, gate_rows, gain_mix).astype(jnp.bfloat16)
    branch = lax.dot_general(
        mixed_out, out_low, (((1,), (1,)), ((), ())), preferred_element_type=jnp.float32
    )
    block_out = tokens_in + branch.reshape(seq_count, length, model_width)
    grad_rows = out_grad.reshape(tok_rows, model_width)
    grad_low = grad_rows.astype(jnp.bfloat16)
    out_weight_grad = lax.dot_general(
        grad_low, mixed_out, (((0,), (0,)), ((), ())), preferred_element_type=jnp.float32
    )
    mixed_grad = lax.dot_general(
        grad_low, out_low, (((1,), (0,)), ((), ())), preferred_element_type=jnp.float32
    )
    gated_value, gated_pull = jax.vjp(gated_apply, ssd_out, gate_rows, gain_mix)
    ssd_grad, gate_grad, mix_gain_grad = gated_pull(mixed_grad)
    gate_grad = gate_grad.astype(jnp.bfloat16)
    gate_weight_grad = lax.dot_general(
        normed, gate_grad, (((0,), (0,)), ((), ())), preferred_element_type=jnp.float32
    )
    out_total = lax.psum_scatter(
        out_weight_grad.astype(jnp.bfloat16), ("dp", "seq"), scatter_dimension=0, tiled=True
    )
    gate_total = lax.psum_scatter(
        gate_weight_grad.astype(jnp.bfloat16), ("dp", "seq"), scatter_dimension=0, tiled=True
    )
    ssd_grad = ssd_grad.reshape(seq_count, length, H, P_SIZE)
    output_value, output_pull = jax.vjp(
        block_output, head_in, b_input, c_output, step_raw, head_params, incoming
    )
    head_in_first, b_first, c_grad, raw_first, params_first, incoming_grad = output_pull(ssd_grad)
    later_grad = earlier_sum(incoming_grad.astype(jnp.bfloat16), after, "seq")
    decay_grad = jnp.sum(later_grad * incoming, axis=(2, 3))
    state_value, state_pull = jax.vjp(state_local, head_in, b_input, step_raw, head_params)
    head_in_second, b_second, raw_second, params_second = state_pull((decay_grad, later_grad))
    mixed_in_grad = jnp.concatenate(
        [
            (head_in_first + head_in_second).reshape(seq_count, length, DI),
            b_first + b_second,
            c_grad,
        ],
        axis=-1,
    )
    conv_value, conv_pull = jax.vjp(conv_apply, extended, conv_taps)
    extended_grad, taps_grad = conv_pull(mixed_in_grad)
    spill_rows = from_behind(
        extended_grad[:, : CONV - 1, :].astype(jnp.bfloat16), "seq", -1
    ).astype(jnp.float32)
    conv_grad = extended_grad[:, CONV - 1 :, :] + jnp.pad(
        spill_rows, ((0, 0), (length - (CONV - 1), 0), (0, 0))
    )
    raw_grad = (raw_first + raw_second).reshape(tok_rows, H)
    rest_grad = jnp.concatenate([conv_grad.reshape(tok_rows, CD), raw_grad], axis=1).astype(
        jnp.bfloat16
    )
    rest_weight_grad = lax.dot_general(
        normed, rest_grad, (((0,), (0,)), ((), ())), preferred_element_type=jnp.float32
    )
    rest_total = lax.psum_scatter(
        rest_weight_grad.astype(jnp.bfloat16), ("dp", "seq"), scatter_dimension=0, tiled=True
    )
    proj_grad = jnp.concatenate([gate_grad, rest_grad], axis=1)
    normed_grad = lax.dot_general(
        proj_grad, in_low, (((1,), (1,)), ((), ())), preferred_element_type=jnp.float32
    )
    norm_value, norm_pull = jax.vjp(norm_apply, flat_tokens, gain_in)
    flat_grad, in_gain_grad = norm_pull(normed_grad)
    tokens_grad = (grad_rows + flat_grad).reshape(seq_count, length, model_width)
    head_grad = params_first + params_second
    pieces = (in_gain_grad, mix_gain_grad, taps_grad.reshape(-1), head_grad.reshape(-1))
    small = jnp.concatenate(pieces)
    spare = -small.shape[0] % 1024
    small = shared_sum(jnp.pad(small, (0, spare)).reshape(-1, 128), ("seq", "dp")).reshape(-1)
    place = lax.axis_index(("dp", "seq"))
    own_gains, own_taps = (norm_gains.shape[0], conv_weight.shape[1])
    taps_at = D + DI
    heads_at = taps_at + taps_grad.size
    gains_total = lax.dynamic_slice(small, (place * own_gains,), (own_gains,))
    taps_total = lax.dynamic_slice(
        small[taps_at:heads_at].reshape(CONV + 1, CD), (0, place * own_taps), (CONV + 1, own_taps)
    )
    head_total = small[heads_at : heads_at + head_grad.size].reshape(head_grad.shape)
    reduced = (
        gains_total,
        jnp.concatenate([gate_total, rest_total], axis=1).astype(jnp.float32),
        taps_total,
        out_total.astype(jnp.float32).T,
    )
    gains_next = adamw_update(norm_gains, reduced[0], gains_first, gains_second, rate_gains)
    in_next = adamw_update(in_weight, reduced[1], in_first, in_second, rate_in)
    conv_next = adamw_update(conv_weight, reduced[2], conv_first, conv_second, rate_conv)
    head_next = adamw_update(head_params, head_total, head_first, head_second, rate_heads)
    out_next = adamw_update(out_weight, reduced[3], out_first, out_second, rate_out)
    return (
        block_out,
        tokens_grad,
        gains_next[0],
        gains_next[1],
        gains_next[2],
        in_next[0],
        in_next[1],
        in_next[2],
        conv_next[0],
        conv_next[1],
        conv_next[2],
        head_next[0],
        head_next[1],
        head_next[2],
        out_next[0],
        out_next[1],
        out_next[2],
    )


def solution(mesh):
    placed = (
        P("dp", "seq", None),
        P("dp", "seq", None),
        P(("dp", "seq")),
        P(("dp", "seq"), None),
        P(None, ("dp", "seq")),
        P(),
        P(None, ("dp", "seq")),
        P(("dp", "seq")),
        P(("dp", "seq")),
        P(("dp", "seq"), None),
        P(("dp", "seq"), None),
        P(None, ("dp", "seq")),
        P(None, ("dp", "seq")),
        P(),
        P(),
        P(None, ("dp", "seq")),
        P(None, ("dp", "seq")),
    )
    return jax.shard_map(
        body,
        mesh=mesh,
        in_specs=placed,
        out_specs=(
            P("dp", "seq", None),
            P("dp", "seq", None),
            P(("dp", "seq")),
            P(("dp", "seq")),
            P(("dp", "seq")),
            P(("dp", "seq"), None),
            P(("dp", "seq"), None),
            P(("dp", "seq"), None),
            P(None, ("dp", "seq")),
            P(None, ("dp", "seq")),
            P(None, ("dp", "seq")),
            P(),
            P(),
            P(),
            P(None, ("dp", "seq")),
            P(None, ("dp", "seq")),
            P(None, ("dp", "seq")),
        ),
        check_vma=False,
    )
```

```python
import jax
import jax.numpy as jnp
from jax import lax
from jax.sharding import PartitionSpec as P

D = 768
H = 24
P_SIZE = 64
N = 128
CONV = 4
STEP = 10
DI = 1536
CD = 1792


norm_eps = 1e-05
beta_one = 0.9
beta_two = 0.999
adam_eps = 1e-08
decay_rate = 0.01
rate_gains = 0.25
rate_in = 0.04
rate_conv = 0.4
rate_heads = 0.6
rate_out = 0.03


def from_behind(value, axis, steps):
    count = lax.axis_size(axis)
    leading, last = (max(0, -steps), min(count, count - steps))
    return lax.ppermute(value, axis, [(source, source + steps) for source in range(leading, last)])


def earlier_sum(state, decays, axis):
    total, factor = (None, None)
    for steps, decay in decays:
        term = from_behind(state, axis, steps).astype(jnp.float32)
        total = term if total is None else total + factor[..., None, None] * term
        factor = decay if factor is None else factor * decay
    return total


def shared_sum(value, axes):
    for axis in axes:
        count, apart = (lax.axis_size(axis), 1)
        while apart < count:
            pairs = [(place, place ^ apart) for place in range(count)]
            value = value + lax.ppermute(value, axis, pairs)
            apart = apart * 2
    return value


def scattered_sum(value, turned):
    dp_bits = lax.axis_size("dp").bit_length() - 1
    seq_bits = lax.axis_size("seq").bit_length() - 1
    dims = [("dp", bit) for bit in reversed(range(dp_bits))]
    dims = dims + [("seq", bit) for bit in reversed(range(seq_bits))]
    near = [("seq", bit) for bit in range(seq_bits)]
    if turned:
        near.reverse()
    order = [("dp", 0)] + near + [("dp", bit) for bit in range(1, dp_bits)]
    columns = value.shape[1]
    for axis, bit in order:
        at = dims.index((axis, bit))
        dims.pop(at)
        halves = value.reshape(2**at, 2, -1, columns)
        own = (lax.axis_index(axis) // 2**bit) % 2
        kept = lax.dynamic_index_in_dim(halves, own, 1, False)
        sent = lax.dynamic_index_in_dim(halves, 1 - own, 1, False)
        pairs = [(place, place ^ 2**bit) for place in range(lax.axis_size(axis))]
        came = lax.ppermute(sent, axis, pairs)
        total = kept.astype(jnp.float32) + came.astype(jnp.float32)
        value = total.astype(jnp.bfloat16).reshape(-1, columns)
    return value


def rounded(values):
    return lax.optimization_barrier(values.astype(jnp.bfloat16)).astype(jnp.float32)


def norm_apply(values, gain):
    return values * lax.rsqrt(jnp.mean(values * values, axis=-1, keepdims=True) + norm_eps) * gain


def gated_apply(ssd_out, gate_rows, gain):
    return norm_apply(ssd_out * jax.nn.silu(gate_rows), gain)


def conv_apply(extended, conv_taps):
    length = extended.shape[1] - (CONV - 1)
    conv_sum = conv_taps[CONV] + conv_taps[0] * extended[:, 0:length]
    for offset in range(1, CONV):
        conv_sum = conv_sum + conv_taps[offset] * extended[:, offset : offset + length]
    return jax.nn.silu(conv_sum)


def block_parts(step_raw, head_params):
    step_size = jax.nn.softplus(step_raw + head_params[0])
    length = step_raw.shape[1]
    row_index = lax.broadcasted_iota(jnp.int32, (length, length), 0)
    col_index = lax.broadcasted_iota(jnp.int32, (length, length), 1)
    until = (col_index <= row_index).astype(jnp.float32)
    cumulative = jnp.einsum(
        "ts,bsh->bth", until, step_size * -jnp.exp(head_params[1]), precision=lax.Precision.HIGHEST
    )
    return (step_size, cumulative)


def state_local(head_in, b_input, step_raw, head_params):
    step_size, cumulative = block_parts(step_raw, head_params)
    weights_end = jnp.exp(cumulative[:, -1:, :] - cumulative) * step_size
    local_state = jnp.einsum(
        "bshp,bsn->bhpn", weights_end[..., None] * head_in, b_input
    )
    return (jnp.exp(cumulative[:, -1, :]), local_state)


def block_output(head_in, b_input, c_output, step_raw, head_params, incoming):
    step_size, cumulative = block_parts(step_raw, head_params)
    length = head_in.shape[1]
    row_index = lax.broadcasted_iota(jnp.int32, (length, length), 0)
    col_index = lax.broadcasted_iota(jnp.int32, (length, length), 1)
    causal = (col_index <= row_index)[None, None]
    cum_heads = jnp.swapaxes(cumulative, 1, 2)
    log_decay = cum_heads[:, :, :, None] - cum_heads[:, :, None, :]
    decay_mask = jnp.exp(jnp.where(causal, log_decay, -1e30))
    inner_bc = jnp.einsum("btn,bsn->bts", c_output, b_input)
    mixing = inner_bc[:, None] * decay_mask * jnp.swapaxes(step_size, 1, 2)[:, :, None, :]
    intra_out = jnp.einsum("bhts,bshp->bthp", mixing, head_in)
    inter_out = jnp.exp(cumulative)[..., None] * jnp.einsum(
        "btn,bhpn->bthp", c_output, incoming
    )
    return intra_out + inter_out + head_params[2][:, None] * head_in


def fetch_weights(norm_gains, in_weight, conv_weight, out_weight):
    axes = ("dp", "seq")
    rows, wide = in_weight.shape
    own_gains = norm_gains.shape[0]
    own_taps = conv_weight.size
    columns = -(-(own_gains + own_taps) // rows)
    small = jnp.concatenate([norm_gains, conv_weight.reshape(-1)])
    small = jnp.pad(small, (0, rows * columns - small.shape[0])).reshape(rows, columns)
    packed = jnp.concatenate([in_weight, small], axis=1).astype(jnp.bfloat16)
    whole = lax.all_gather(packed, axes, axis=0, tiled=True)
    out_low = lax.all_gather(out_weight.astype(jnp.bfloat16).T, axes, axis=0, tiled=True)
    count = whole.shape[0] // rows
    small_all = whole[:, wide:].reshape(count, rows * columns)
    gain_all = small_all[:, :own_gains].reshape(-1)
    taps = small_all[:, own_gains : own_gains + own_taps].reshape(count, CONV + 1, -1)
    conv_taps = jnp.swapaxes(taps, 0, 1).reshape(CONV + 1, -1)
    return (gain_all, whole[:, :wide], conv_taps, out_low)


def adamw_update(weight, gradient, first_moment, second_moment, step_rate):
    first_next = beta_one * first_moment + (1.0 - beta_one) * gradient
    second_next = beta_two * second_moment + (1.0 - beta_two) * gradient * gradient
    first_hat = first_next / (1.0 - beta_one**STEP)
    second_hat = second_next / (1.0 - beta_two**STEP)
    weight_next = weight - step_rate * (
        first_hat / (jnp.sqrt(second_hat) + adam_eps) + decay_rate * weight
    )
    return (first_next, second_next, weight_next)


def body(
    tokens_in,
    out_grad,
    norm_gains,
    in_weight,
    conv_weight,
    head_params,
    out_weight,
    gains_first,
    gains_second,
    in_first,
    in_second,
    conv_first,
    conv_second,
    head_first,
    head_second,
    out_first,
    out_second,
):
    seq_count, length, model_width = tokens_in.shape
    tok_rows = seq_count * length
    fetched = fetch_weights(norm_gains, in_weight, conv_weight, out_weight)
    gain_all = fetched[0].astype(jnp.float32)
    in_low = fetched[1]
    conv_taps = fetched[2].astype(jnp.float32)
    out_low = fetched[3]
    gain_in = gain_all[:D]
    gain_mix = gain_all[D:]
    flat_tokens = tokens_in.reshape(tok_rows, model_width)
    normed = norm_apply(flat_tokens, gain_in).astype(jnp.bfloat16)
    projected = jnp.dot(normed, in_low, preferred_element_type=jnp.float32).astype(jnp.bfloat16)
    gate_rows = projected[:, :DI].astype(jnp.float32)
    conv_in = projected[:, DI : DI + CD].reshape(seq_count, length, CD)
    step_raw = projected[:, DI + CD :].astype(jnp.float32).reshape(seq_count, length, H)
    tail_rows = conv_in[:, length - (CONV - 1) :, :]
    before_rows = from_behind(tail_rows, "seq", 1)
    extended = jnp.concatenate([before_rows, conv_in], axis=1).astype(jnp.float32)
    mixed_in = rounded(conv_apply(extended, conv_taps))
    head_in = mixed_in[..., :DI].reshape(seq_count, length, H, P_SIZE)
    b_input = mixed_in[..., DI : DI + N]
    c_output = mixed_in[..., DI + N :]
    decay_end, local_state = state_local(head_in, b_input, step_raw, head_params)
    peers = lax.axis_size("seq")
    before = [(k, from_behind(decay_end, "seq", k)) for k in range(1, peers)]
    after = [(-k, from_behind(decay_end, "seq", -k)) for k in range(1, peers)]
    incoming = earlier_sum(local_state.astype(jnp.bfloat16), before, "seq")
    ssd_out = block_output(head_in, b_input, c_output, step_raw, head_params, incoming).reshape(
        tok_rows, DI
    )
    mixed_out = gated_apply(ssd_out, gate_rows, gain_mix).astype(jnp.bfloat16)
    branch = lax.dot_general(
        mixed_out, out_low, (((1,), (1,)), ((), ())), preferred_element_type=jnp.float32
    )
    block_out = tokens_in + branch.reshape(seq_count, length, model_width)
    grad_rows = out_grad.reshape(tok_rows, model_width)
    grad_low = grad_rows.astype(jnp.bfloat16)
    out_weight_grad = lax.dot_general(
        grad_low, mixed_out, (((0,), (0,)), ((), ())), preferred_element_type=jnp.float32
    )
    mixed_grad = lax.dot_general(
        grad_low, out_low, (((1,), (0,)), ((), ())), preferred_element_type=jnp.float32
    )
    gated_value, gated_pull = jax.vjp(gated_apply, ssd_out, gate_rows, gain_mix)
    ssd_grad, gate_grad, mix_gain_grad = gated_pull(mixed_grad)
    gate_grad = gate_grad.astype(jnp.bfloat16)
    gate_weight_grad = lax.dot_general(
        normed, gate_grad, (((0,), (0,)), ((), ())), preferred_element_type=jnp.float32
    )
    out_total = scattered_sum(out_weight_grad.astype(jnp.bfloat16), False)
    gate_total = scattered_sum(gate_weight_grad.astype(jnp.bfloat16), True)
    ssd_grad = ssd_grad.reshape(seq_count, length, H, P_SIZE)
    output_value, output_pull = jax.vjp(
        block_output, head_in, b_input, c_output, step_raw, head_params, incoming
    )
    head_in_first, b_first, c_grad, raw_first, params_first, incoming_grad = output_pull(ssd_grad)
    later_grad = earlier_sum(incoming_grad.astype(jnp.bfloat16), after, "seq")
    decay_grad = jnp.sum(later_grad * incoming, axis=(2, 3))
    state_value, state_pull = jax.vjp(state_local, head_in, b_input, step_raw, head_params)
    head_in_second, b_second, raw_second, params_second = state_pull((decay_grad, later_grad))
    mixed_in_grad = jnp.concatenate(
        [
            (head_in_first + head_in_second).reshape(seq_count, length, DI),
            b_first + b_second,
            c_grad,
        ],
        axis=-1,
    )
    conv_value, conv_pull = jax.vjp(conv_apply, extended, conv_taps)
    extended_grad, taps_grad = conv_pull(mixed_in_grad)
    spill_rows = from_behind(
        extended_grad[:, : CONV - 1, :].astype(jnp.bfloat16), "seq", -1
    ).astype(jnp.float32)
    conv_grad = extended_grad[:, CONV - 1 :, :] + jnp.pad(
        spill_rows, ((0, 0), (length - (CONV - 1), 0), (0, 0))
    )
    raw_grad = (raw_first + raw_second).reshape(tok_rows, H)
    rest_grad = jnp.concatenate([conv_grad.reshape(tok_rows, CD), raw_grad], axis=1).astype(
        jnp.bfloat16
    )
    rest_weight_grad = lax.dot_general(
        normed, rest_grad, (((0,), (0,)), ((), ())), preferred_element_type=jnp.float32
    )
    rest_low = rest_weight_grad.astype(jnp.bfloat16)
    rest_totals = [
        scattered_sum(rest_low[:, :1024], False),
        scattered_sum(rest_low[:, 1024:], True),
    ]
    proj_grad = jnp.concatenate([gate_grad, rest_grad], axis=1)
    normed_grad = lax.dot_general(
        proj_grad, in_low, (((1,), (1,)), ((), ())), preferred_element_type=jnp.float32
    )
    norm_value, norm_pull = jax.vjp(norm_apply, flat_tokens, gain_in)
    flat_grad, in_gain_grad = norm_pull(normed_grad)
    tokens_grad = (grad_rows + flat_grad).reshape(seq_count, length, model_width)
    head_grad = params_first + params_second
    pieces = (in_gain_grad, mix_gain_grad, taps_grad.reshape(-1), head_grad.reshape(-1))
    small = jnp.concatenate(pieces)
    spare = -small.shape[0] % 1024
    small = shared_sum(jnp.pad(small, (0, spare)).reshape(-1, 128), ("seq", "dp")).reshape(-1)
    place = lax.axis_index(("dp", "seq"))
    own_gains, own_taps = (norm_gains.shape[0], conv_weight.shape[1])
    taps_at = D + DI
    heads_at = taps_at + taps_grad.size
    gains_total = lax.dynamic_slice(small, (place * own_gains,), (own_gains,))
    taps_total = lax.dynamic_slice(
        small[taps_at:heads_at].reshape(CONV + 1, CD), (0, place * own_taps), (CONV + 1, own_taps)
    )
    head_total = small[heads_at : heads_at + head_grad.size].reshape(head_grad.shape)
    reduced = (
        gains_total,
        jnp.concatenate([gate_total] + rest_totals, axis=1).astype(jnp.float32),
        taps_total,
        out_total.astype(jnp.float32).T,
    )
    gains_next = adamw_update(norm_gains, reduced[0], gains_first, gains_second, rate_gains)
    in_next = adamw_update(in_weight, reduced[1], in_first, in_second, rate_in)
    conv_next = adamw_update(conv_weight, reduced[2], conv_first, conv_second, rate_conv)
    head_next = adamw_update(head_params, head_total, head_first, head_second, rate_heads)
    out_next = adamw_update(out_weight, reduced[3], out_first, out_second, rate_out)
    return (
        block_out,
        tokens_grad,
        gains_next[0],
        gains_next[1],
        gains_next[2],
        in_next[0],
        in_next[1],
        in_next[2],
        conv_next[0],
        conv_next[1],
        conv_next[2],
        head_next[0],
        head_next[1],
        head_next[2],
        out_next[0],
        out_next[1],
        out_next[2],
    )


def solution(mesh):
    placed = (
        P("dp", "seq", None),
        P("dp", "seq", None),
        P(("dp", "seq")),
        P(("dp", "seq"), None),
        P(None, ("dp", "seq")),
        P(),
        P(None, ("dp", "seq")),
        P(("dp", "seq")),
        P(("dp", "seq")),
        P(("dp", "seq"), None),
        P(("dp", "seq"), None),
        P(None, ("dp", "seq")),
        P(None, ("dp", "seq")),
        P(),
        P(),
        P(None, ("dp", "seq")),
        P(None, ("dp", "seq")),
    )
    return jax.shard_map(
        body,
        mesh=mesh,
        in_specs=placed,
        out_specs=(
            P("dp", "seq", None),
            P("dp", "seq", None),
            P(("dp", "seq")),
            P(("dp", "seq")),
            P(("dp", "seq")),
            P(("dp", "seq"), None),
            P(("dp", "seq"), None),
            P(("dp", "seq"), None),
            P(None, ("dp", "seq")),
            P(None, ("dp", "seq")),
            P(None, ("dp", "seq")),
            P(),
            P(),
            P(),
            P(None, ("dp", "seq")),
            P(None, ("dp", "seq")),
            P(None, ("dp", "seq")),
        ),
        check_vma=False,
    )
```
